32 devices in a mesh: groups: 2 (over y), gx: 4 (over z), gy: 2 (over x), gz: 2 (over core).
Axes of the slice: x: 2, y: 2, z: 4, core: 2. Of those that a mesh axis runs over, the one named last changes fastest.
Arguments:
- prompt_rows: bfloat16 [1024, 8192], P(('groups', 'gx', 'gz'), 'gy'), parts along dimension 0, may hold values from -6 to 6
- gate_up: bfloat16 [8192, 2, 28672], P('gy', None, ('gx', 'gz')), may hold values from -0.0625 to 0.0625
- queries: bfloat16 [2, 128, 8192], P(None, ('groups', 'gy'), ('gx', 'gz')), parts along dimension 1, may hold values from -128 to 128
- new_kv: bfloat16 [2, 128, 1024], P(None, ('groups', 'gy')), parts along dimension 1, may hold values from -6 to 6
- kv_cache: bfloat16 [128, 2048, 1024], P(('groups', 'gy'), ('gx', 'gz')), parts along dimension 0, may hold values from -6 to 6
- lengths: int32 [128], P(('groups', 'gy')), parts along dimension 0, may hold values from 2 to 2048, as said below
Outputs:
- hidden_units: bfloat16 [1024, 28672], P(('groups', 'gy'), ('gx', 'gz')), parts along dimension 0
- attended: bfloat16 [2, 128, 8192], P(None, ('groups', 'gy'), ('gx', 'gz')), parts along dimension 1
The draws below stay inside these ranges and needn't reach their ends.
There are 2 independent parts, one for each index of `groups`. The reference program is written for one: setup_inputs(seed, part) draws one part's arguments, and reference() takes and returns one part's arrays. A program takes and returns all parts, laid end to end along the dimension named above; an argument that names none is the same for every part. Nothing has to cross between parts.
Inputs may be any that keep to these rules, and one draw needn't show every extreme that they name: Slots 0 to lengths[b] - 1 of sequence b are live; some sequence has exactly 2048.
All inputs are finite; a program needn't handle non-finite values.
Results may differ from the reference program's by a relative error of at most 0.024.
Values may be sent and summed in bfloat16 or wider, within the bound.
No kernel may reach another device: no remote copies, remote signals or barrier semaphores. Data moves between devices by JAX's collectives and lax.ppermute only.
A program may use at most 256 MiB of HBM per device.

```python
import math
import jax
import jax.numpy as jnp
from jax import lax

DW = 8192
FW = 28672
H = 64
KVH = 4
HD = 128
S = 2
B = 64
P_SIZE = 512
L = 2048
N_GY = 2


def front_slots(key):
    base_key = jax.random.fold_in(key, 12)
    leading = jnp.clip(jax.random.normal(base_key, (B, 2, 2, KVH, HD), jnp.float32), -6.0, 6.0)
    return leading


def draw_kv_cache(key, part):
    leading = front_slots(key)
    later_key = jax.random.fold_in(key, 13)
    remainder = jnp.clip(jax.random.normal(later_key, (B, L - 2, 2, KVH, HD), jnp.float32), -6.0, 6.0)
    complete = jnp.concatenate([leading, remainder], axis=1)
    return complete.reshape(B, L, 2 * KVH * HD).astype(jnp.bfloat16)


def draw_queries(key, part):
    drawn = jnp.clip(jax.random.normal(jax.random.fold_in(key, 14), (S, B, H * HD), jnp.float32), -6.0, 6.0)
    return drawn.astype(jnp.bfloat16)


def draw_lengths(key, part):
    base_key = jax.random.fold_in(key, 21)
    spread = jax.random.randint(jax.random.fold_in(base_key, 1), (B,), 2, L + 1)
    shorter = jax.random.randint(jax.random.fold_in(base_key, 2), (B,), 2, 17)
    picker = jax.random.randint(jax.random.fold_in(base_key, 3), (B,), 0, 8)
    chosen = jnp.where(picker == 0, shorter, spread)
    longest = jax.random.randint(jax.random.fold_in(base_key, 4), (), 0, B)
    return chosen.at[longest].set(L).astype(jnp.int32)


def level_of(key, dims, cuts, low, high):
    level, own = 1.0, jax.random.fold_in(key, 6)
    for axis_at, blocks in cuts:
        heights = jnp.exp(jax.random.uniform(jax.random.fold_in(own, axis_at), (blocks,), jnp.float32, low / len(cuts), high / len(cuts)))
        level = level * jnp.repeat(heights, dims[axis_at] // blocks).reshape([-1 if axis == axis_at else 1 for axis in range(len(dims))])
    return level


def bell_draw(key, shape, deviation, bound, split=(), kind=jnp.bfloat16):
    loudness = level_of(key, shape, split, -0.22, 0.18) if split else 1.0
    values = jax.random.normal(key, shape, jnp.float32) * deviation * loudness
    return jnp.minimum(jnp.maximum(values, -bound), bound).astype(kind)


def setup_inputs(seed: int = 0, part: int = 0) -> dict:
    key_list = jax.random.split(jax.random.key(seed), 7)
    own_keys = jax.random.split(jax.random.fold_in(key_list[6], part), 7)
    return {
        "prompt_rows": bell_draw(own_keys[0], (P_SIZE, DW), 1.0, 6.0, ((0, 8), (1, 2))),
        "gate_up": bell_draw(key_list[1], (DW, 2, FW), DW ** -0.5, 0.0625, ((0, 2), (2, 8))),
        "queries": draw_queries(jax.random.fold_in(jax.random.fold_in(key_list[6], part), 71), part),
        "new_kv": bell_draw(own_keys[3], (S, B, 2 * KVH * HD), 1.0, 6.0, ((1, 2),)),
        "kv_cache": draw_kv_cache(jax.random.fold_in(jax.random.fold_in(key_list[6], part), 71), part),
        "lengths": draw_lengths(jax.random.fold_in(jax.random.fold_in(key_list[6], part), 71), part),
    }


def one_sequence(inputs):
    seq_queries, fresh_kv, cache_rows, length = inputs
    combined = jnp.concatenate([cache_rows, fresh_kv], axis=0).reshape(L + S, 2, KVH, HD)
    key_rows = combined[:, 0].astype(jnp.float32)
    value_rows = combined[:, 1].astype(jnp.float32)
    grouped = seq_queries.reshape(S, KVH, H // KVH, HD).astype(jnp.float32)
    scores = jnp.einsum('skgd,jkd->skgj', grouped, key_rows) * (1.0 / math.sqrt(HD))
    position = jnp.arange(L + S, dtype=jnp.int32)
    step_ids = jnp.arange(S, dtype=jnp.int32)
    visible = (position[None, :] < length) | (position[None, :] >= L) & (position[None, :] - L <= step_ids[:, None])
    masked = jnp.where(visible[:, None, None, :], scores, -jnp.inf)
    row_max = lax.optimization_barrier(jnp.max(masked, axis=-1, keepdims=True))
    probabilities = jnp.exp(masked - row_max)
    denominator = lax.optimization_barrier(jnp.sum(probabilities, axis=-1, keepdims=True))
    weights = lax.optimization_barrier(probabilities.astype(jnp.bfloat16)).astype(jnp.float32)
    numerator = jnp.einsum('skgj,jkd->skgd', weights, value_rows)
    return (numerator / denominator).reshape(S, H * HD).astype(jnp.bfloat16)

def reference(prompt_rows, gate_up, queries, new_kv, kv_cache, lengths):
    block_width = DW // N_GY
    flat_weights = gate_up.reshape(DW, 2 * FW)
    summed = jnp.zeros((prompt_rows.shape[0], 2 * FW), jnp.float32)
    for member in range(N_GY):
        lower = member * block_width
        partial_value = jnp.dot(prompt_rows[:, lower:lower + block_width], flat_weights[lower:lower + block_width], preferred_element_type=jnp.float32)
        rounded = lax.optimization_barrier(partial_value.astype(jnp.bfloat16))
        summed = summed + rounded.astype(jnp.float32)
    summed = summed.reshape(-1, 2, FW)
    hidden_units = (jax.nn.silu(summed[:, 0]) * summed[:, 1]).astype(jnp.bfloat16)
    attended = lax.map(one_sequence, (jnp.transpose(queries, (1, 0, 2)), jnp.transpose(new_kv, (1, 0, 2)), kv_cache, lengths))
    return (hidden_units, jnp.transpose(attended, (1, 0, 2)))
```

```python
import functools
import math

import jax
import jax.numpy as jnp
from jax import lax
from jax.experimental import pallas as pl
from jax.experimental.pallas import tpu as pltpu
from jax.sharding import PartitionSpec as P

KVH = 4
HD = 128
lowest = -1e30
f32 = jnp.float32
bf16 = jnp.bfloat16
SHORT = pl.CostEstimate(flops=1, bytes_accessed=1, transcendentals=0)


def xor_pairs(axis, bit):
    return [(i, i ^ bit) for i in range(lax.axis_size(axis))]


def both_cores(x):
    other = lax.ppermute(x, "gz", [(0, 1), (1, 0)])
    first = lax.axis_index("gz") == 0
    return jnp.where(first, x, other), jnp.where(first, other, x)


def attention_kernel(limits_ref, *refs, per_step, members):
    q_ref, kv_ref, num_ref, stat_ref = refs[-4:]
    rows = q_ref.shape[2]
    slots = kv_ref.shape[1]
    half = kv_ref.shape[2] // 2
    total = members * rows
    share = members // KVH
    step = pl.program_id(0)
    slot = lax.broadcasted_iota(jnp.int32, (slots, total), 0)
    zero = jnp.zeros((rows * share, HD), bf16)
    for i in range(per_step):
        limit = limits_ref[step * per_step + i]
        wide = []
        for k in range(KVH):
            mine = jnp.concatenate([q_ref[k * share + m, i] for m in range(share)], axis=0)
            wide.append(jnp.concatenate([mine if j == k else zero for j in range(KVH)], axis=1))
        wide = jnp.concatenate(wide, axis=0)
        scores = lax.dot_general(
            kv_ref[i, :, :half], wide, (((1,), (1,)), ((), ())), preferred_element_type=f32
        ) * (1.0 / math.sqrt(HD))
        seen = slot < limit
        scores = jnp.where(seen, scores, lowest)
        top = jnp.max(scores, axis=0, keepdims=True)
        probs = jnp.where(seen, jnp.exp(scores - top), 0.0)
        stat_ref[0, i : i + 1, :] = top
        stat_ref[1, i : i + 1, :] = jnp.sum(probs, axis=0, keepdims=True)
        weights = probs.T.astype(bf16)
        full = jnp.dot(weights, kv_ref[i, :, half:], preferred_element_type=f32)
        for m in range(members):
            k = m // share
            num_ref[m, i] = full[m * rows : (m + 1) * rows, k * HD : (k + 1) * HD].astype(bf16)


def cached_attention(all_q, kv_cache, limits, *tokens):
    members, sequences, rows, _ = all_q.shape
    slots, width = kv_cache.shape[1:]
    per_step = 8
    total = members * rows
    return pl.pallas_call(
        functools.partial(attention_kernel, per_step=per_step, members=members),
        grid_spec=pltpu.PrefetchScalarGridSpec(
            num_scalar_prefetch=1,
            grid=(sequences // per_step,),
            in_specs=[pl.BlockSpec(memory_space=pl.ANY)] * len(tokens)
            + [
                pl.BlockSpec((members, per_step, rows, HD), lambda j, _: (0, j, 0, 0)),
                pl.BlockSpec((per_step, slots, width), lambda j, _: (j, 0, 0)),
            ],
            out_specs=[
                pl.BlockSpec((members, per_step, rows, HD), lambda j, _: (0, j, 0, 0)),
                pl.BlockSpec((2, per_step, total), lambda j, _: (0, j, 0)),
            ],
        ),
        out_shape=[
            jax.ShapeDtypeStruct((members, sequences, rows, HD), bf16),
            jax.ShapeDtypeStruct((2, sequences, total), f32),
        ],
        compiler_params=pltpu.CompilerParams(vmem_limit_bytes=40 << 20),
        cost_estimate=SHORT,
    )(limits, *tokens, all_q, kv_cache)


def lane_kernel(x_ref, out_ref):
    half = x_ref.shape[1] // 2
    row = lax.broadcasted_iota(jnp.int32, (256, 256), 0)
    col = lax.broadcasted_iota(jnp.int32, (256, 256), 1)
    place = (col == 2 * (row % 128) + row // 128).astype(f32).astype(bf16)
    for c in range(half // 128):
        both = jnp.concatenate(
            [x_ref[:, c * 128 : (c + 1) * 128], x_ref[:, half + c * 128 : half + (c + 1) * 128]],
            axis=1,
        )
        moved = jnp.dot(both, place, preferred_element_type=f32)
        out_ref[:, c * 256 : (c + 1) * 256] = moved.astype(bf16)


def interleave_lanes(x):
    return pl.pallas_call(
        lane_kernel,
        out_shape=jax.ShapeDtypeStruct(x.shape, bf16),
        cost_estimate=SHORT,
    )(x)


def split_rows(first, second):
    rows = first.shape[0]
    odd = (lax.broadcasted_iota(jnp.int32, (1, 8, 128), 1) & 1) == 1
    a = first.astype(f32).reshape(rows // 8, 8, 128)
    b = second.astype(f32).reshape(rows // 8, 8, 128)
    gate = jnp.where(odd, pltpu.roll(b, 1, 1), a)
    up = jnp.where(odd, b, pltpu.roll(a, 7, 1))
    return gate.reshape(rows, 128).astype(bf16), up.reshape(rows, 128).astype(bf16)


def product_kernel(*refs, count, cuts):
    x_ref, left_ref, right_ref = refs[-5 - len(cuts) : -2 - len(cuts)]
    outs, (flat, sems) = refs[-2 - len(cuts) : -2], refs[-2:]
    j = pl.program_id(0)
    depth = left_ref.shape[0]
    piece = min(1024, depth)
    halves = [r.reshape(2 * depth, 128) for r in (left_ref, right_ref)]

    def copies(slot):
        return [
            pltpu.make_async_copy(h, flat.at[slot, t], sems.at[slot, t])
            for t, h in enumerate(halves)
        ]

    @pl.when(j < count)
    def _():
        for c in copies(lax.rem(j, 2)):
            c.start()

    @pl.when(j > 0)
    def _():
        slot = lax.rem(j + 1, 2)
        rows = x_ref.shape[0]
        gate = up = jnp.zeros((rows, 256), f32)
        for i in range(0, depth, piece):
            sides = [
                split_rows(flat[slot, t, i : i + piece], flat[slot, t, depth + i : depth + i + piece])
                for t in range(2)
            ]
            x = x_ref[:, i : i + piece]
            gate += jnp.dot(
                x, jnp.concatenate([s[0] for s in sides], 1), preferred_element_type=f32
            )
            up += jnp.dot(x, jnp.concatenate([s[1] for s in sides], 1), preferred_element_type=f32)
        low = 0
        for ref, high in zip(outs, cuts):
            ref[0] = gate[low:high].astype(bf16)
            ref[1] = up[low:high].astype(bf16)
            low = high

    @pl.when(j < count)
    def _():
        for c in copies(lax.rem(j, 2)):
            c.wait()


def product(x, weights, first, last, cuts, *tokens):
    rows, depth = x.shape
    count = last - first
    sizes = [high - low for low, high in zip((0,) + cuts[:-1], cuts)]
    return pl.pallas_call(
        functools.partial(product_kernel, count=count, cuts=cuts),
        grid=(count + 1,),
        in_specs=[pl.BlockSpec(memory_space=pl.ANY)] * len(tokens)
        + [
            pl.BlockSpec((rows, depth), lambda j: (0, 0)),
            pl.BlockSpec(
                (depth, 1, 2, 128), lambda j: (0, 2 * (first + jnp.minimum(j, count - 1)), 0, 0)
            ),
            pl.BlockSpec(
                (depth, 1, 2, 128), lambda j: (0, 2 * (first + jnp.minimum(j, count - 1)) + 1, 0, 0)
            ),
        ],
        out_specs=[
            pl.BlockSpec((2, size, 256), lambda j: (0, 0, jnp.maximum(j - 1, 0))) for size in sizes
        ],
        out_shape=[jax.ShapeDtypeStruct((2, size, count * 256), bf16) for size in sizes],
        scratch_shapes=[
            pltpu.VMEM((2, 2, 2 * depth, 128), bf16),
            pltpu.SemaphoreType.DMA((2, 2)),
        ],
        compiler_params=pltpu.CompilerParams(vmem_limit_bytes=48 << 20),
        cost_estimate=SHORT,
    )(*tokens, x, weights, weights)


def gated_kernel(swap_ref, held_ref, kept_ref, near_ref, far_ref, out_ref):
    half = near_ref.shape[1]
    for i, theirs in enumerate((near_ref, far_ref)):
        rows = slice(i * half, (i + 1) * half)
        gate = kept_ref[0, rows].astype(f32) + theirs[0].astype(f32)
        up = kept_ref[1, rows].astype(f32) + theirs[1].astype(f32)
        start = jnp.bitwise_xor(swap_ref[0], i) * half
        out_ref[pl.ds(pl.multiple_of(start, half), half), :] = (jax.nn.silu(gate) * up).astype(bf16)


def gated(kept, near, far, swap, held, first, width):
    rows, half, columns = kept.shape[1], near.shape[1], kept.shape[2]
    wide = 512 if columns % 512 == 0 and first % 2 == 0 else 256
    return pl.pallas_call(
        gated_kernel,
        grid_spec=pltpu.PrefetchScalarGridSpec(
            num_scalar_prefetch=1,
            grid=(columns // wide,),
            in_specs=[
                pl.BlockSpec(memory_space=pl.ANY),
                pl.BlockSpec((2, rows, wide), lambda j, _: (0, 0, j)),
                pl.BlockSpec((2, half, wide), lambda j, _: (0, 0, j)),
                pl.BlockSpec((2, half, wide), lambda j, _: (0, 0, j)),
            ],
            out_specs=pl.BlockSpec((rows, wide), lambda j, _: (0, first * 256 // wide + j)),
        ),
        out_shape=jax.ShapeDtypeStruct((rows, width), bf16),
        input_output_aliases={} if held is None else {1: 0},
        cost_estimate=SHORT,
    )(swap, kept if held is None else held, kept, near, far)


def merge(terms):
    top = functools.reduce(jnp.maximum, [t[1] for t in terms])
    scales = [jnp.exp(t[1] - top) for t in terms]
    num = sum(t[0].astype(f32) * s[..., None] for t, s in zip(terms, scales))
    den = sum(t[2] * s for t, s in zip(terms, scales))
    return num, top, den


def new_token_terms(q, new_kv, kv_head, steps):
    sequences = q.shape[0]
    units = new_kv.reshape(steps, sequences, 2 * KVH, HD)
    keys = lax.dynamic_index_in_dim(units, kv_head, 2, False).astype(f32)
    values = lax.dynamic_index_in_dim(units, kv_head + KVH, 2, False).astype(f32)
    heads = q.shape[1] // steps
    step_of = jnp.arange(q.shape[1], dtype=jnp.int32) // heads
    qf = q.astype(f32)
    scores = [
        jnp.sum(qf * keys[t][:, None, :], axis=-1) * (1.0 / math.sqrt(HD)) for t in range(steps)
    ]
    scores = [jnp.where(t <= step_of[None, :], s, lowest) for t, s in enumerate(scores)]
    top = functools.reduce(jnp.maximum, scores)
    probs = [
        jnp.where(t <= step_of[None, :], jnp.exp(s - top), 0.0) for t, s in enumerate(scores)
    ]
    num = sum(
        p.astype(bf16).astype(f32)[..., None] * values[t][:, None, :] for t, p in enumerate(probs)
    )
    return num, top, sum(probs)


def on_device(prompt_rows, gate_up, queries, new_kv, kv_cache, lengths):
    gx, gy, gz = (lax.axis_index(a) for a in ("gx", "gy", "gz"))
    chips = lax.axis_size("gx")
    cores = lax.axis_size("gz")
    depth, _, width = gate_up.shape
    block = prompt_rows.shape[0]
    to_send = (gx // 2) != gy

    mine = interleave_lanes(prompt_rows)
    over_two = lax.ppermute(mine, "gx", xor_pairs("gx", 2))
    send_near = jnp.where(to_send, mine, over_two)
    own_near = jnp.where(to_send, over_two, mine)
    send_far = lax.ppermute(send_near, "gx", xor_pairs("gx", 1))
    own_far = lax.ppermute(own_near, "gx", xor_pairs("gx", 1))
    x1 = jnp.concatenate(both_cores(send_near), axis=0)
    x2 = jnp.concatenate(
        both_cores(send_far) + both_cores(own_near) + both_cores(own_far), axis=0
    )

    steps = queries.shape[0]
    sequences, slots = kv_cache.shape[:2]
    members = chips * cores
    me = gx * cores + gz
    heads = queries.shape[2] // HD
    my_q = queries.reshape(steps, sequences, heads, HD).transpose(1, 0, 2, 3)
    my_q = my_q.reshape(sequences, steps * heads, HD)
    late = over_two[0, 0]
    queued = my_q + jnp.where(late != late, late, jnp.zeros_like(late))
    all_q = lax.all_gather(queued, ("gx", "gz"), axis=0)

    weights = gate_up.reshape(depth, 2, width // 128, 128).transpose(0, 2, 1, 3)
    pairs = width // 256
    cuts = [0, pairs // 14 * 4, pairs // 14 * 10, pairs] if pairs % 14 == 0 else [0, pairs]
    spans = list(zip(cuts[:-1], cuts[1:]))
    over = [(0, 1), (1, 0)]
    half = cores * block
    near, tokens = [], ()
    for first, last in spans:
        (out,) = product(x1, weights, first, last, (half,), *tokens)
        near.append(lax.ppermute(out, "gy", over))
        tokens = (out,)
    limits = jnp.clip(lengths - me * slots, 0, slots)
    kept, far = [], []
    for i, (first, last) in enumerate(spans):
        arrived = far[i - 2] if i >= 2 else near[i]
        if i == len(spans) - 1:
            num, stat = cached_attention(all_q, kv_cache, limits, *tokens, near[-1])
            tokens = (num,)
        sent, keep = product(x2, weights, first, last, (half, 3 * half), *tokens, arrived)
        far.append(lax.ppermute(sent, "gy", over))
        kept.append(keep)
        tokens = (keep,)
    swap = (gx % 2).reshape(1)
    hidden_units = None
    for i, (first, last) in enumerate(spans):
        hidden_units = gated(kept[i], near[i], far[i], swap, hidden_units, first, width)

    rows = steps * heads
    num = num.reshape(chips, cores, sequences, rows, HD)
    stat = stat.reshape(2, sequences, chips, cores, rows).transpose(2, 3, 0, 1, 4)
    keep_num = lax.dynamic_index_in_dim(num, gz, 1, False)
    give_num = lax.dynamic_index_in_dim(num, 1 - gz, 1, False)
    keep_stat = lax.dynamic_index_in_dim(stat, gz, 1, False)
    give_stat = lax.dynamic_index_in_dim(stat, 1 - gz, 1, False)
    got_num = lax.ppermute(give_num, "gz", over)
    got_stat = lax.ppermute(give_stat, "gz", over)
    pair_num, pair_top, pair_den = merge(
        [(keep_num, keep_stat[:, 0], keep_stat[:, 1]), (got_num, got_stat[:, 0], got_stat[:, 1])]
    )
    pair_num = pair_num.astype(bf16)
    pair_stat = jnp.stack([pair_top, pair_den], axis=1)
    terms = []
    for bit in range(chips):
        n = lax.dynamic_index_in_dim(pair_num, gx ^ bit, 0, False)
        s = lax.dynamic_index_in_dim(pair_stat, gx ^ bit, 0, False)
        if bit:
            n = lax.ppermute(n, "gx", xor_pairs("gx", bit))
            s = lax.ppermute(s, "gx", xor_pairs("gx", bit))
        terms.append((n, s[0], s[1]))
    terms.append(new_token_terms(my_q, new_kv, me * KVH // members, steps))
    num, _, den = merge(terms)
    attended = (num / den[..., None]).astype(bf16)
    attended = attended.reshape(sequences, steps, heads, HD).transpose(1, 0, 2, 3)
    return hidden_units, attended.reshape(steps, sequences, heads * HD)


def plain_on_device(prompt_rows, gate_up, queries, new_kv, kv_cache, lengths):
    partial_terms = jnp.dot(
        lax.all_gather(prompt_rows, ("gx", "gz"), axis=0, tiled=True),
        gate_up.reshape(gate_up.shape[0], -1),
        preferred_element_type=f32,
    )
    summed = lax.psum_scatter(
        partial_terms.astype(bf16), "gy", scatter_dimension=0, tiled=True
    ).astype(f32)
    summed = summed.reshape(summed.shape[0], 2, -1)
    hidden_units = (jax.nn.silu(summed[:, 0]) * summed[:, 1]).astype(bf16)
    members = lax.axis_size(("gx", "gz"))
    me = lax.axis_index(("gx", "gz"))
    steps = queries.shape[0]
    sequences, slots = kv_cache.shape[:2]
    all_q = lax.all_gather(queries, ("gx", "gz"), axis=2, tiled=True)
    grouped = all_q.reshape(steps, sequences, KVH, -1, HD)
    cache = kv_cache.reshape(sequences, slots, 2, KVH, HD)
    fresh = new_kv.reshape(steps, sequences, 2, KVH, HD).transpose(1, 0, 2, 3, 4)
    units = jnp.concatenate([cache, fresh], axis=1)
    scores = jnp.einsum(
        "sukgd,ujkd->sukgj", grouped, units[:, :, 0], preferred_element_type=f32
    ) * (1.0 / math.sqrt(HD))
    cached = me * slots + jnp.arange(slots, dtype=jnp.int32)[None, :] < lengths[:, None]
    ids = jnp.arange(steps, dtype=jnp.int32)
    fresh_seen = (ids[None, :] <= ids[:, None]) & (me == 0)
    seen = jnp.concatenate(
        [
            jnp.broadcast_to(cached[None], (steps, sequences, slots)),
            jnp.broadcast_to(fresh_seen[:, None, :], (steps, sequences, steps)),
        ],
        axis=2,
    )[:, :, None, None, :]
    masked = jnp.where(seen, scores, lowest)
    top = jnp.max(masked, axis=-1)
    probs = jnp.where(seen, jnp.exp(masked - top[..., None]), 0.0)
    den = jnp.sum(probs, axis=-1)
    num = jnp.einsum(
        "sukgj,ujkd->sukgd", probs.astype(bf16), units[:, :, 1], preferred_element_type=f32
    )
    overall = lax.pmax(top, ("gx", "gz"))
    scale = jnp.exp(top - overall)
    num = (num * scale[..., None]).reshape(steps, sequences, -1, HD)
    den = (den * scale).reshape(steps, sequences, -1)
    num = lax.psum_scatter(
        num.astype(bf16), ("gx", "gz"), scatter_dimension=2, tiled=True
    ).astype(f32)
    den = lax.psum_scatter(den, ("gx", "gz"), scatter_dimension=2, tiled=True)
    attended = (num / den[..., None]).astype(bf16)
    return hidden_units, attended.reshape(steps, sequences, -1)


def solution(mesh):
    sizes = mesh.shape
    paired = sizes["gy"] == 2 and sizes["gx"] == KVH and sizes["gz"] == 2
    return jax.shard_map(
        on_device if paired else plain_on_device,
        mesh=mesh,
        in_specs=(
            P(("groups", "gx", "gz"), "gy"),
            P("gy", None, ("gx", "gz")),
            P(None, ("groups", "gy"), ("gx", "gz")),
            P(None, ("groups", "gy"), None),
            P(("groups", "gy"), ("gx", "gz"), None),
            P(("groups", "gy")),
        ),
        out_specs=(P(("groups", "gy"), ("gx", "gz")), P(None, ("groups", "gy"), ("gx", "gz"))),
        check_vma=False,
    )
```

```python
import functools
import math

import jax
import jax.numpy as jnp
from jax import lax
from jax.experimental import pallas as pl
from jax.experimental.pallas import tpu as pltpu
from jax.sharding import PartitionSpec as P

KVH = 4
HD = 128
lowest = -1e30
f32 = jnp.float32
bf16 = jnp.bfloat16
VMEM = 44 << 20
SHORT = pl.CostEstimate(flops=1, bytes_accessed=1, transcendentals=0)


def xor_pairs(axis, bit):
    return [(i, i ^ bit) for i in range(lax.axis_size(axis))]


def after(x, *tokens):
    anywhere = pl.BlockSpec(memory_space=pl.ANY)
    return pl.pallas_call(
        lambda *refs: None,
        in_specs=[anywhere] * (1 + len(tokens)),
        out_specs=anywhere,
        out_shape=jax.ShapeDtypeStruct(x.shape, x.dtype),
        input_output_aliases={0: 0},
        cost_estimate=SHORT,
    )(x, *tokens)


def attention_kernel(limits_ref, place_ref, mine_ref, other_ref, kv_ref, num_ref, stat_ref):
    chips, per_step, rows, _ = mine_ref.shape
    slots = kv_ref.shape[1]
    half = kv_ref.shape[2] // 2
    total = 2 * chips * rows
    step = pl.program_id(0)
    gx, gz = place_ref[0], place_ref[1]
    slot = lax.broadcasted_iota(jnp.int32, (slots, total), 0)
    zero = jnp.zeros((2 * rows, HD), bf16)
    tops, sums = [], []
    for i in range(per_step):
        limit = limits_ref[step * per_step + i]
        wide = []
        for k in range(KVH):
            mine = mine_ref[k ^ gx, i]
            other = other_ref[k ^ gx, i]
            pair = jnp.concatenate(
                [jnp.where(gz == 0, mine, other), jnp.where(gz == 0, other, mine)], axis=0
            )
            wide.append(jnp.concatenate([pair if j == k else zero for j in range(KVH)], axis=1))
        wide = jnp.concatenate(wide, axis=0)
        scores = lax.dot_general(
            kv_ref[i, :, :half], wide, (((1,), (1,)), ((), ())), preferred_element_type=f32
        ) * (1.0 / math.sqrt(HD))
        seen = slot < limit
        scores = jnp.where(seen, scores, lowest)
        top = jnp.max(scores, axis=0, keepdims=True)
        probs = jnp.where(seen, jnp.exp(scores - top), 0.0)
        tops.append(top)
        sums.append(jnp.sum(probs, axis=0, keepdims=True))
        weights = probs.T.astype(bf16)
        full = jnp.dot(weights, kv_ref[i, :, half:], preferred_element_type=f32).astype(bf16)
        for k in range(KVH):
            for z in range(2):
                low = (2 * k + z) * rows
                num_ref[z ^ gz, k ^ gx, i] = full[low : low + rows, k * HD : (k + 1) * HD]
    for n, parts in enumerate((tops, sums)):
        joined = jnp.concatenate(parts, axis=0)
        for k in range(KVH):
            for z in range(2):
                low = (2 * k + z) * rows
                stat_ref[z ^ gz, k ^ gx, n] = joined[:, low : low + rows]


def cached_attention(mine, other, kv_cache, limits, place):
    chips, sequences, rows, _ = mine.shape
    slots, width = kv_cache.shape[1:]
    per_step = 8
    return pl.pallas_call(
        attention_kernel,
        grid_spec=pltpu.PrefetchScalarGridSpec(
            num_scalar_prefetch=2,
            grid=(sequences // per_step,),
            in_specs=[
                pl.BlockSpec((chips, per_step, rows, HD), lambda j, *_: (0, j, 0, 0)),
                pl.BlockSpec((chips, per_step, rows, HD), lambda j, *_: (0, j, 0, 0)),
                pl.BlockSpec((per_step, slots, width), lambda j, *_: (j, 0, 0)),
            ],
            out_specs=[
                pl.BlockSpec((2, chips, per_step, rows, HD), lambda j, *_: (0, 0, j, 0, 0)),
                pl.BlockSpec((2, chips, 2, per_step, rows), lambda j, *_: (0, 0, 0, j, 0)),
            ],
        ),
        out_shape=[
            jax.ShapeDtypeStruct((2, chips, sequences, rows, HD), bf16),
            jax.ShapeDtypeStruct((2, chips, 2, sequences, rows), f32),
        ],
        compiler_params=pltpu.CompilerParams(vmem_limit_bytes=VMEM),
        cost_estimate=SHORT,
    )(limits, place, mine, other, kv_cache)


def thirds(x):
    parts = []
    for _ in range(3):
        parts.append(x.astype(bf16))
        x = x - parts[-1].astype(f32)
    return parts


def pair_kernel(num_ref, other_num_ref, stat_ref, other_stat_ref, out_ref):
    chips, sequences = num_ref.shape[1:3]
    for c in range(chips):
        top = jnp.maximum(stat_ref[0, c, 0], other_stat_ref[c, 0])
        left = jnp.exp(stat_ref[0, c, 0] - top)
        right = jnp.exp(other_stat_ref[c, 0] - top)
        total = stat_ref[0, c, 1] * left + other_stat_ref[c, 1] * right
        parts = thirds(top) + thirds(total)
        parts.append(jnp.zeros((sequences, HD - 6 * parts[0].shape[1]), bf16))
        packed = jnp.concatenate(parts, axis=1)
        rows = out_ref.shape[2]
        for n in range(sequences // rows):
            out_ref[c, sequences + n] = packed[n * rows : (n + 1) * rows]
        left, right = left.T, right.T
        for b in range(sequences):
            out_ref[c, b] = (
                num_ref[0, c, b].astype(f32) * left[:, b : b + 1]
                + other_num_ref[c, b].astype(f32) * right[:, b : b + 1]
            ).astype(bf16)


def join_pair(num, other_num, stat, other_stat):
    first = pl.BlockSpec((1,) + num.shape[1:], lambda j: (0, 0, 0, 0, 0))
    first_stat = pl.BlockSpec((1,) + stat.shape[1:], lambda j: (0, 0, 0, 0, 0))
    rest = pl.BlockSpec(num.shape[1:], lambda j: (0, 0, 0, 0))
    rest_stat = pl.BlockSpec(stat.shape[1:], lambda j: (0, 0, 0, 0))
    _, chips, sequences, rows, _ = num.shape
    out_shape = (chips, sequences + sequences // rows, rows, HD)
    return pl.pallas_call(
        pair_kernel,
        grid=(1,),
        in_specs=[first, rest, first_stat, rest_stat],
        out_specs=pl.BlockSpec(out_shape, lambda j: (0, 0, 0, 0)),
        out_shape=jax.ShapeDtypeStruct(out_shape, bf16),
        compiler_params=pltpu.CompilerParams(vmem_limit_bytes=VMEM),
        cost_estimate=SHORT,
    )(num, other_num, stat, other_stat)


def final_kernel(*refs, count):
    nums = refs[:count]
    q_ref, key_ref, value_ref, out_ref = refs[count:]
    sequences, rows, _ = q_ref.shape
    steps = key_ref.shape[0]
    scale = 1.0 / math.sqrt(HD)
    stats = []
    for r in nums:
        packed = jnp.concatenate([r[b] for b in range(sequences, r.shape[0])], axis=0).astype(f32)
        parts = [packed[:, n * rows : (n + 1) * rows] for n in range(6)]
        stats.append([(sum(parts[n + 1 : n + 3], parts[n])).T for n in (0, 3)])
    step_of = lax.broadcasted_iota(jnp.int32, (rows, 1), 0) // (rows // steps)
    for b in range(sequences):
        q = q_ref[b].astype(f32)
        fresh = []
        for t in range(steps):
            key = key_ref[t, b : b + 1, :].astype(f32)
            score = jnp.sum(q * key, axis=1, keepdims=True) * scale
            fresh.append(jnp.where(step_of >= t, score, lowest))
        tops = [s[0][:, b : b + 1] for s in stats]
        top = functools.reduce(jnp.maximum, tops + fresh)
        num = jnp.zeros((rows, HD), f32)
        den = jnp.zeros((rows, 1), f32)
        for t in range(steps):
            prob = jnp.where(step_of >= t, jnp.exp(fresh[t] - top), 0.0)
            den += prob
            num += prob.astype(bf16).astype(f32) * value_ref[t, b : b + 1, :].astype(f32)
        for n, s, m in zip(nums, stats, tops):
            part = jnp.exp(m - top)
            den += part * s[1][:, b : b + 1]
            num += part * n[b].astype(f32)
        out_ref[b] = (num / den).astype(bf16)


def join_all(nums, q, keys, values):
    return pl.pallas_call(
        functools.partial(final_kernel, count=len(nums)),
        out_shape=jax.ShapeDtypeStruct(q.shape, bf16),
        cost_estimate=SHORT,
    )(*nums, q, keys, values)


def lane_kernel(x_ref, out_ref):
    half = x_ref.shape[1] // 2
    row = lax.broadcasted_iota(jnp.int32, (256, 256), 0)
    col = lax.broadcasted_iota(jnp.int32, (256, 256), 1)
    place = (col == 2 * (row % 128) + row // 128).astype(f32).astype(bf16)
    for c in range(half // 128):
        both = jnp.concatenate(
            [x_ref[:, c * 128 : (c + 1) * 128], x_ref[:, half + c * 128 : half + (c + 1) * 128]],
            axis=1,
        )
        moved = jnp.dot(both, place, preferred_element_type=f32)
        out_ref[:, c * 256 : (c + 1) * 256] = moved.astype(bf16)


def interleave_lanes(x):
    return pl.pallas_call(
        lane_kernel,
        out_shape=jax.ShapeDtypeStruct(x.shape, bf16),
        cost_estimate=SHORT,
    )(x)


def split_rows(first, second):
    rows = first.shape[0]
    odd = (lax.broadcasted_iota(jnp.int32, (1, 8, 128), 1) & 1) == 1
    a = first.astype(f32).reshape(rows // 8, 8, 128)
    b = second.astype(f32).reshape(rows // 8, 8, 128)
    gate = jnp.where(odd, pltpu.roll(b, 1, 1), a)
    up = jnp.where(odd, b, pltpu.roll(a, 7, 1))
    return gate.reshape(rows, 128).astype(bf16), up.reshape(rows, 128).astype(bf16)


def product_kernel(place_ref, *refs, count, cuts, pieces):
    x_ref, sems, x_sems, flat = refs[-4:]
    outs = refs[-4 - len(cuts) : -4]
    left_ref, right_ref = refs[-6 - len(cuts) : -4 - len(cuts)]
    block = x_ref.shape[0] // (2 * len(pieces))
    gz, to_send = place_ref[1], place_ref[2]
    j = pl.program_id(0)
    depth = left_ref.shape[0]
    piece = min(1024, depth)
    halves = [r.reshape(2 * depth, 128) for r in (left_ref, right_ref)]

    def copies(slot):
        return [
            pltpu.make_async_copy(h, flat.at[slot, t], sems.at[slot, t])
            for t, h in enumerate(halves)
        ]

    def fetch(act, chosen):
        for p, sources in enumerate(pieces):
            for core, source in enumerate(sources[chosen]):
                start = pl.multiple_of((2 * p + jnp.bitwise_xor(gz, core)) * block, block)
                act(
                    pltpu.make_async_copy(
                        refs[source], x_ref.at[pl.ds(start, block)], x_sems.at[p, core]
                    )
                )

    @pl.when((j == 0) & (to_send == 1))
    def _():
        fetch(lambda c: c.start(), 0)

    @pl.when((j == 0) & (to_send == 0))
    def _():
        fetch(lambda c: c.start(), 1)

    @pl.when(j < count)
    def _():
        for c in copies(lax.rem(j, 2)):
            c.start()

    @pl.when(j > 0)
    def _():
        slot = lax.rem(j + 1, 2)
        rows = x_ref.shape[0]
        gate = up = jnp.zeros((rows, 256), f32)
        for i in range(0, depth, piece):
            sides = [
                split_rows(flat[slot, t, i : i + piece], flat[slot, t, depth + i : depth + i + piece])
                for t in range(2)
            ]
            x = x_ref[:, i : i + piece]
            gate += jnp.dot(
                x, jnp.concatenate([s[0] for s in sides], 1), preferred_element_type=f32
            )
            up += jnp.dot(x, jnp.concatenate([s[1] for s in sides], 1), preferred_element_type=f32)
        low = 0
        for ref, high in zip(outs, cuts):
            ref[0] = gate[low:high].astype(bf16)
            ref[1] = up[low:high].astype(bf16)
            low = high

    @pl.when(j < count)
    def _():
        for c in copies(lax.rem(j, 2)):
            c.wait()

    @pl.when(j == 0)
    def _():
        fetch(lambda c: c.wait(), 0)


def product(place, blocks, pieces, weights, first, last, cuts, *tokens):
    block, depth = blocks[0].shape
    rows = 2 * len(pieces) * block
    count = last - first
    sizes = [high - low for low, high in zip((0,) + cuts[:-1], cuts)]
    anywhere = [pl.BlockSpec(memory_space=pl.ANY)]
    stay = [pl.BlockSpec(memory_space=pltpu.HBM)]

    def column(side):
        return pl.BlockSpec(
            (depth, 1, 2, 128),
            lambda j, _: (0, 2 * (first + jnp.minimum(j, count - 1)) + side, 0, 0),
        )

    return pl.pallas_call(
        functools.partial(product_kernel, count=count, cuts=cuts, pieces=pieces),
        grid_spec=pltpu.PrefetchScalarGridSpec(
            num_scalar_prefetch=1,
            grid=(count + 1,),
            in_specs=anywhere * len(blocks) + stay * len(tokens) + [column(0), column(1)],
            out_specs=[
                pl.BlockSpec((2, size, 256), lambda j, _: (0, 0, jnp.maximum(j - 1, 0)))
                for size in sizes
            ],
            scratch_shapes=[
                pltpu.VMEM((rows, depth), bf16),
                pltpu.SemaphoreType.DMA((2, 2)),
                pltpu.SemaphoreType.DMA((len(pieces), 2)),
                pltpu.VMEM((2, 2, 2 * depth, 128), bf16),
            ],
        ),
        out_shape=[jax.ShapeDtypeStruct((2, size, count * 256), bf16) for size in sizes],
        compiler_params=pltpu.CompilerParams(vmem_limit_bytes=VMEM),
        cost_estimate=SHORT,
    )(place, *blocks, *tokens, weights, weights)


def gated_kernel(swap_ref, held_ref, kept_ref, near_ref, far_ref, out_ref):
    half = near_ref.shape[1]
    for i, theirs in enumerate((near_ref, far_ref)):
        rows = slice(i * half, (i + 1) * half)
        gate = kept_ref[0, rows].astype(f32) + theirs[0].astype(f32)
        up = kept_ref[1, rows].astype(f32) + theirs[1].astype(f32)
        start = jnp.bitwise_xor(swap_ref[0], i) * half
        out_ref[pl.ds(pl.multiple_of(start, half), half), :] = (jax.nn.silu(gate) * up).astype(bf16)


def gated(kept, near, far, swap, held, first, width):
    rows, half, columns = kept.shape[1], near.shape[1], kept.shape[2]
    wide = 512 if columns % 512 == 0 and first % 2 == 0 else 256
    return pl.pallas_call(
        gated_kernel,
        grid_spec=pltpu.PrefetchScalarGridSpec(
            num_scalar_prefetch=1,
            grid=(columns // wide,),
            in_specs=[
                pl.BlockSpec(memory_space=pl.ANY),
                pl.BlockSpec((2, rows, wide), lambda j, _: (0, 0, j)),
                pl.BlockSpec((2, half, wide), lambda j, _: (0, 0, j)),
                pl.BlockSpec((2, half, wide), lambda j, _: (0, 0, j)),
            ],
            out_specs=pl.BlockSpec((rows, wide), lambda j, _: (0, first * 256 // wide + j)),
        ),
        out_shape=jax.ShapeDtypeStruct((rows, width), bf16),
        input_output_aliases={} if held is None else {1: 0},
        cost_estimate=SHORT,
    )(swap, kept if held is None else held, kept, near, far)


def on_device(prompt_rows, gate_up, queries, new_kv, kv_cache, lengths):
    gx, gy, gz = (lax.axis_index(a) for a in ("gx", "gy", "gz"))
    chips = lax.axis_size("gx")
    cores = lax.axis_size("gz")
    depth, _, width = gate_up.shape
    block = prompt_rows.shape[0]
    to_send = ((gx // 2) != gy).astype(jnp.int32)
    place = jnp.stack([gx, gz, to_send])
    over = [(0, 1), (1, 0)]

    mine = interleave_lanes(prompt_rows)
    along = lax.ppermute(mine, "gx", xor_pairs("gx", 2))
    mine_far = lax.ppermute(mine, "gx", xor_pairs("gx", 1))
    mine_other = lax.ppermute(mine, "gz", over)

    steps = queries.shape[0]
    sequences, slots = kv_cache.shape[:2]
    me = gx * cores + gz
    heads = queries.shape[2] // HD
    rows = steps * heads
    my_q = queries.reshape(steps, sequences, heads, HD).transpose(1, 0, 2, 3)
    my_q = after(my_q.reshape(1, sequences, rows, HD), mine)
    all_q = jnp.concatenate(
        [my_q] + [lax.ppermute(my_q, "gx", xor_pairs("gx", bit)) for bit in range(1, chips)], axis=0
    )
    other_q = lax.ppermute(all_q, "gz", over)
    limits = jnp.clip(lengths - me * slots, 0, slots)
    num, stat = cached_attention(all_q, other_q, kv_cache, limits, place)

    along = after(along, num)
    along_other = lax.ppermute(along, "gz", over)
    along_far = lax.ppermute(along, "gx", xor_pairs("gx", 1))
    mine_far_other = lax.ppermute(mine_far, "gz", over)
    along_far_other = lax.ppermute(along_far, "gz", over)

    other_num = lax.ppermute(num[1], "gz", over)
    other_stat = lax.ppermute(stat[1], "gz", over)
    pair = join_pair(num, other_num, stat, other_stat)
    nums = [pair[0]]
    for bit in range(1, chips):
        nums.append(lax.ppermute(pair[bit], "gx", xor_pairs("gx", bit)))
    units = new_kv.reshape(steps, sequences, 2 * KVH, HD)
    keys = lax.dynamic_index_in_dim(units, gx, 2, False)
    values = lax.dynamic_index_in_dim(units, gx + KVH, 2, False)
    attended = join_all(nums, my_q[0], keys, values)

    weights = gate_up.reshape(depth, 2, width // 128, 128).transpose(0, 2, 1, 3)
    pairs = width // 256
    cuts = [0, pairs // 14 * 4, pairs // 14 * 10, pairs] if pairs % 14 == 0 else [0, pairs]
    spans = list(zip(cuts[:-1], cuts[1:]))
    half = cores * block
    swap = (gx % 2).reshape(1)
    near, tokens = [], (num,)
    blocks = (mine, mine_other, along, along_other)
    pieces = (((0, 1), (2, 3)),)
    for i, (first, last) in enumerate(spans):
        (out,) = product(place, blocks, pieces, weights, first, last, (half,), *tokens)
        near.append(lax.ppermute(out, "gy", over))
        tokens = (out, pair)
    blocks += (mine_far, mine_far_other, along_far, along_far_other)
    pieces = (((4, 5), (6, 7)), ((2, 3), (0, 1)), ((6, 7), (4, 5)))
    tokens = (out, near[0])
    hidden_units = None
    waiting = []
    for i, (first, last) in enumerate(spans):
        sent, keep = product(place, blocks, pieces, weights, first, last, (half, 3 * half), *tokens)
        waiting.append((keep, near[i], lax.ppermute(sent, "gy", over), first))
        tokens = (keep, near[min(i + 1, len(near) - 1)], *nums[1:])
        if i + 1 >= len(spans) - 1 and len(waiting) > 1:
            keep, early, late, start = waiting.pop(0)
            hidden_units = gated(keep, early, late, swap, hidden_units, start, width)
            tokens += (hidden_units,)
    for keep, early, late, start in waiting:
        hidden_units = gated(keep, early, late, swap, hidden_units, start, width)

    attended = attended.reshape(sequences, steps, heads, HD).transpose(1, 0, 2, 3)
    return hidden_units, attended.reshape(steps, sequences, heads * HD)


def plain_on_device(prompt_rows, gate_up, queries, new_kv, kv_cache, lengths):
    partial_terms = jnp.dot(
        lax.all_gather(prompt_rows, ("gx", "gz"), axis=0, tiled=True),
        gate_up.reshape(gate_up.shape[0], -1),
        preferred_element_type=f32,
    )
    summed = lax.psum_scatter(
        partial_terms.astype(bf16), "gy", scatter_dimension=0, tiled=True
    ).astype(f32)
    summed = summed.reshape(summed.shape[0], 2, -1)
    hidden_units = (jax.nn.silu(summed[:, 0]) * summed[:, 1]).astype(bf16)
    members = lax.axis_size(("gx", "gz"))
    me = lax.axis_index(("gx", "gz"))
    steps = queries.shape[0]
    sequences, slots = kv_cache.shape[:2]
    all_q = lax.all_gather(queries, ("gx", "gz"), axis=2, tiled=True)
    grouped = all_q.reshape(steps, sequences, KVH, -1, HD)
    cache = kv_cache.reshape(sequences, slots, 2, KVH, HD)
    fresh = new_kv.reshape(steps, sequences, 2, KVH, HD).transpose(1, 0, 2, 3, 4)
    units = jnp.concatenate([cache, fresh], axis=1)
    scores = jnp.einsum(
        "sukgd,ujkd->sukgj", grouped, units[:, :, 0], preferred_element_type=f32
    ) * (1.0 / math.sqrt(HD))
    cached = me * slots + jnp.arange(slots, dtype=jnp.int32)[None, :] < lengths[:, None]
    ids = jnp.arange(steps, dtype=jnp.int32)
    fresh_seen = (ids[None, :] <= ids[:, None]) & (me == 0)
    seen = jnp.concatenate(
        [
            jnp.broadcast_to(cached[None], (steps, sequences, slots)),
            jnp.broadcast_to(fresh_seen[:, None, :], (steps, sequences, steps)),
        ],
        axis=2,
    )[:, :, None, None, :]
    masked = jnp.where(seen, scores, lowest)
    top = jnp.max(masked, axis=-1)
    probs = jnp.where(seen, jnp.exp(masked - top[..., None]), 0.0)
    den = jnp.sum(probs, axis=-1)
    num = jnp.einsum(
        "sukgj,ujkd->sukgd", probs.astype(bf16), units[:, :, 1], preferred_element_type=f32
    )
    overall = lax.pmax(top, ("gx", "gz"))
    scale = jnp.exp(top - overall)
    num = (num * scale[..., None]).reshape(steps, sequences, -1, HD)
    den = (den * scale).reshape(steps, sequences, -1)
    num = lax.psum_scatter(
        num.astype(bf16), ("gx", "gz"), scatter_dimension=2, tiled=True
    ).astype(f32)
    den = lax.psum_scatter(den, ("gx", "gz"), scatter_dimension=2, tiled=True)
    attended = (num / den[..., None]).astype(bf16)
    return hidden_units, attended.reshape(steps, sequences, -1)


def solution(mesh):
    sizes = mesh.shape
    paired = sizes["gy"] == 2 and sizes["gx"] == KVH and sizes["gz"] == 2
    return jax.shard_map(
        on_device if paired else plain_on_device,
        mesh=mesh,
        in_specs=(
            P(("groups", "gx", "gz"), "gy"),
            P("gy", None, ("gx", "gz")),
            P(None, ("groups", "gy"), ("gx", "gz")),
            P(None, ("groups", "gy"), None),
            P(("groups", "gy"), ("gx", "gz"), None),
            P(("groups", "gy")),
        ),
        out_specs=(P(("groups", "gy"), ("gx", "gz")), P(None, ("groups", "gy"), ("gx", "gz"))),
        check_vma=False,
    )
```

```python
import functools
import math

import jax
import jax.numpy as jnp
from jax import lax
from jax.experimental import pallas as pl
from jax.experimental.pallas import tpu as pltpu
from jax.sharding import PartitionSpec as P

KVH = 4
HD = 128
lowest = -1e30
f32 = jnp.float32
bf16 = jnp.bfloat16
VMEM = 44 << 20
TOKEN = jax.ShapeDtypeStruct((8, 128), jnp.float32)
SHORT = pl.CostEstimate(flops=1, bytes_accessed=1, transcendentals=0)


def xor_pairs(axis, bit):
    return [(i, i ^ bit) for i in range(lax.axis_size(axis))]


def after(x, *tokens):
    anywhere = pl.BlockSpec(memory_space=pl.ANY)
    return pl.pallas_call(
        lambda *refs: None,
        in_specs=[anywhere] * (1 + len(tokens)),
        out_specs=anywhere,
        out_shape=jax.ShapeDtypeStruct(x.shape, x.dtype),
        input_output_aliases={0: 0},
        cost_estimate=SHORT,
    )(x, *tokens)


def token_spec():
    return pl.BlockSpec(TOKEN.shape, lambda *_: (0, 0))


def attention_kernel(
    limits_ref, place_ref, mine_ref, other_ref, kv_ref, num_ref, stat_ref, token_ref
):
    chips, per_step, rows, _ = mine_ref.shape
    slots = kv_ref.shape[1]
    half = kv_ref.shape[2] // 2
    total = 2 * chips * rows
    step = pl.program_id(0)
    gx, gz = place_ref[0], place_ref[1]
    slot = lax.broadcasted_iota(jnp.int32, (slots, total), 0)
    zero = jnp.zeros((2 * rows, HD), bf16)
    token_ref[...] = jnp.zeros_like(token_ref)
    tops, sums = [], []
    for i in range(per_step):
        limit = limits_ref[step * per_step + i]
        wide = []
        for k in range(KVH):
            mine = mine_ref[k ^ gx, i]
            other = other_ref[k ^ gx, i]
            pair = jnp.concatenate(
                [jnp.where(gz == 0, mine, other), jnp.where(gz == 0, other, mine)], axis=0
            )
            wide.append(jnp.concatenate([pair if j == k else zero for j in range(KVH)], axis=1))
        wide = jnp.concatenate(wide, axis=0)
        scores = lax.dot_general(
            kv_ref[i, :, :half], wide, (((1,), (1,)), ((), ())), preferred_element_type=f32
        ) * (1.0 / math.sqrt(HD))
        seen = slot < limit
        scores = jnp.where(seen, scores, lowest)
        top = jnp.max(scores, axis=0, keepdims=True)
        probs = jnp.where(seen, jnp.exp(scores - top), 0.0)
        tops.append(top)
        sums.append(jnp.sum(probs, axis=0, keepdims=True))
        weights = probs.T.astype(bf16)
        full = jnp.dot(weights, kv_ref[i, :, half:], preferred_element_type=f32).astype(bf16)
        for k in range(KVH):
            for z in range(2):
                low = (2 * k + z) * rows
                num_ref[z ^ gz, k ^ gx, i] = full[low : low + rows, k * HD : (k + 1) * HD]
    for n, parts in enumerate((tops, sums)):
        joined = jnp.concatenate(parts, axis=0)
        for k in range(KVH):
            for z in range(2):
                low = (2 * k + z) * rows
                stat_ref[z ^ gz, k ^ gx, n] = joined[:, low : low + rows]


def cached_attention(mine, other, kv_cache, limits, place):
    chips, sequences, rows, _ = mine.shape
    slots, width = kv_cache.shape[1:]
    per_step = 8
    return pl.pallas_call(
        attention_kernel,
        grid_spec=pltpu.PrefetchScalarGridSpec(
            num_scalar_prefetch=2,
            grid=(sequences // per_step,),
            in_specs=[
                pl.BlockSpec((chips, per_step, rows, HD), lambda j, *_: (0, j, 0, 0)),
                pl.BlockSpec((chips, per_step, rows, HD), lambda j, *_: (0, j, 0, 0)),
                pl.BlockSpec((per_step, slots, width), lambda j, *_: (j, 0, 0)),
            ],
            out_specs=[
                pl.BlockSpec((2, chips, per_step, rows, HD), lambda j, *_: (0, 0, j, 0, 0)),
                pl.BlockSpec((2, chips, 2, per_step, rows), lambda j, *_: (0, 0, 0, j, 0)),
                token_spec(),
            ],
        ),
        out_shape=[
            jax.ShapeDtypeStruct((2, chips, sequences, rows, HD), bf16),
            jax.ShapeDtypeStruct((2, chips, 2, sequences, rows), f32),
            TOKEN,
        ],
        compiler_params=pltpu.CompilerParams(vmem_limit_bytes=VMEM),
        cost_estimate=SHORT,
    )(limits, place, mine, other, kv_cache)


def thirds(x):
    parts = []
    for _ in range(3):
        parts.append(x.astype(bf16))
        x = x - parts[-1].astype(f32)
    return parts


def pair_kernel(num_ref, other_num_ref, stat_ref, other_stat_ref, out_ref, token_ref):
    chips, sequences = num_ref.shape[1:3]
    token_ref[...] = jnp.zeros_like(token_ref)
    for c in range(chips):
        top = jnp.maximum(stat_ref[0, c, 0], other_stat_ref[c, 0])
        left = jnp.exp(stat_ref[0, c, 0] - top)
        right = jnp.exp(other_stat_ref[c, 0] - top)
        total = stat_ref[0, c, 1] * left + other_stat_ref[c, 1] * right
        parts = thirds(top) + thirds(total)
        parts.append(jnp.zeros((sequences, HD - 6 * parts[0].shape[1]), bf16))
        packed = jnp.concatenate(parts, axis=1)
        rows = out_ref.shape[2]
        for n in range(sequences // rows):
            out_ref[c, sequences + n] = packed[n * rows : (n + 1) * rows]
        left, right = left.T, right.T
        for b in range(sequences):
            out_ref[c, b] = (
                num_ref[0, c, b].astype(f32) * left[:, b : b + 1]
                + other_num_ref[c, b].astype(f32) * right[:, b : b + 1]
            ).astype(bf16)


def join_pair(num, other_num, stat, other_stat):
    first = pl.BlockSpec((1,) + num.shape[1:], lambda j: (0, 0, 0, 0, 0))
    first_stat = pl.BlockSpec((1,) + stat.shape[1:], lambda j: (0, 0, 0, 0, 0))
    rest = pl.BlockSpec(num.shape[1:], lambda j: (0, 0, 0, 0))
    rest_stat = pl.BlockSpec(stat.shape[1:], lambda j: (0, 0, 0, 0))
    _, chips, sequences, rows, _ = num.shape
    out_shape = (chips, sequences + sequences // rows, rows, HD)
    return pl.pallas_call(
        pair_kernel,
        grid=(1,),
        in_specs=[first, rest, first_stat, rest_stat],
        out_specs=[pl.BlockSpec(out_shape, lambda j: (0, 0, 0, 0)), token_spec()],
        out_shape=[jax.ShapeDtypeStruct(out_shape, bf16), TOKEN],
        compiler_params=pltpu.CompilerParams(vmem_limit_bytes=VMEM),
        cost_estimate=SHORT,
    )(num, other_num, stat, other_stat)


def final_kernel(*refs, count):
    nums = refs[:count]
    q_ref, key_ref, value_ref, out_ref = refs[count:]
    sequences, rows, _ = q_ref.shape
    steps = key_ref.shape[0]
    scale = 1.0 / math.sqrt(HD)
    stats = []
    for r in nums:
        packed = jnp.concatenate([r[b] for b in range(sequences, r.shape[0])], axis=0).astype(f32)
        parts = [packed[:, n * rows : (n + 1) * rows] for n in range(6)]
        stats.append([(sum(parts[n + 1 : n + 3], parts[n])).T for n in (0, 3)])
    step_of = lax.broadcasted_iota(jnp.int32, (rows, 1), 0) // (rows // steps)
    for b in range(sequences):
        q = q_ref[b].astype(f32)
        fresh = []
        for t in range(steps):
            key = key_ref[t, b : b + 1, :].astype(f32)
            score = jnp.sum(q * key, axis=1, keepdims=True) * scale
            fresh.append(jnp.where(step_of >= t, score, lowest))
        tops = [s[0][:, b : b + 1] for s in stats]
        top = functools.reduce(jnp.maximum, tops + fresh)
        num = jnp.zeros((rows, HD), f32)
        den = jnp.zeros((rows, 1), f32)
        for t in range(steps):
            prob = jnp.where(step_of >= t, jnp.exp(fresh[t] - top), 0.0)
            den += prob
            num += prob.astype(bf16).astype(f32) * value_ref[t, b : b + 1, :].astype(f32)
        for n, s, m in zip(nums, stats, tops):
            part = jnp.exp(m - top)
            den += part * s[1][:, b : b + 1]
            num += part * n[b].astype(f32)
        out_ref[b] = (num / den).astype(bf16)


def join_all(nums, q, keys, values):
    return pl.pallas_call(
        functools.partial(final_kernel, count=len(nums)),
        out_shape=jax.ShapeDtypeStruct(q.shape, bf16),
        cost_estimate=SHORT,
    )(*nums, q, keys, values)


def lane_kernel(x_ref, out_ref):
    half = x_ref.shape[1] // 2
    row = lax.broadcasted_iota(jnp.int32, (256, 256), 0)
    col = lax.broadcasted_iota(jnp.int32, (256, 256), 1)
    place = (col == 2 * (row % 128) + row // 128).astype(f32).astype(bf16)
    for c in range(half // 128):
        both = jnp.concatenate(
            [x_ref[:, c * 128 : (c + 1) * 128], x_ref[:, half + c * 128 : half + (c + 1) * 128]],
            axis=1,
        )
        moved = jnp.dot(both, place, preferred_element_type=f32)
        out_ref[:, c * 256 : (c + 1) * 256] = moved.astype(bf16)


def interleave_lanes(x):
    return pl.pallas_call(
        lane_kernel,
        out_shape=jax.ShapeDtypeStruct(x.shape, bf16),
        cost_estimate=SHORT,
    )(x)


def split_rows(first, second):
    rows = first.shape[0]
    odd = (lax.broadcasted_iota(jnp.int32, (1, 8, 128), 1) & 1) == 1
    a = first.astype(f32).reshape(rows // 8, 8, 128)
    b = second.astype(f32).reshape(rows // 8, 8, 128)
    gate = jnp.where(odd, pltpu.roll(b, 1, 1), a)
    up = jnp.where(odd, b, pltpu.roll(a, 7, 1))
    return gate.reshape(rows, 128).astype(bf16), up.reshape(rows, 128).astype(bf16)


def product_kernel(place_ref, *refs, count, cuts, pieces):
    token_ref, x_ref, sems, x_sems, flat = refs[-5:]
    outs = refs[-5 - len(cuts) : -5]
    left_ref, right_ref = refs[-7 - len(cuts) : -5 - len(cuts)]
    block = x_ref.shape[0] // (2 * len(pieces))
    gz, to_send = place_ref[1], place_ref[2]
    j = pl.program_id(0)
    depth = left_ref.shape[0]
    piece = min(1024, depth)
    halves = [r.reshape(2 * depth, 128) for r in (left_ref, right_ref)]

    def copies(slot):
        return [
            pltpu.make_async_copy(h, flat.at[slot, t], sems.at[slot, t])
            for t, h in enumerate(halves)
        ]

    def fetch(act, chosen):
        for p, sources in enumerate(pieces):
            for core, source in enumerate(sources[chosen]):
                start = pl.multiple_of((2 * p + jnp.bitwise_xor(gz, core)) * block, block)
                act(
                    pltpu.make_async_copy(
                        refs[source], x_ref.at[pl.ds(start, block)], x_sems.at[p, core]
                    )
                )

    @pl.when((j == 0) & (to_send == 1))
    def _():
        fetch(lambda c: c.start(), 0)

    @pl.when((j == 0) & (to_send == 0))
    def _():
        fetch(lambda c: c.start(), 1)

    @pl.when(j < count)
    def _():
        for c in copies(lax.rem(j, 2)):
            c.start()

    @pl.when(j > 0)
    def _():
        slot = lax.rem(j + 1, 2)
        rows = x_ref.shape[0]
        gate = up = jnp.zeros((rows, 256), f32)
        for i in range(0, depth, piece):
            sides = [
                split_rows(flat[slot, t, i : i + piece], flat[slot, t, depth + i : depth + i + piece])
                for t in range(2)
            ]
            x = x_ref[:, i : i + piece]
            gate += jnp.dot(
                x, jnp.concatenate([s[0] for s in sides], 1), preferred_element_type=f32
            )
            up += jnp.dot(x, jnp.concatenate([s[1] for s in sides], 1), preferred_element_type=f32)
        token_ref[...] = jnp.zeros_like(token_ref)
        low = 0
        for ref, high in zip(outs, cuts):
            ref[0] = gate[low:high].astype(bf16)
            ref[1] = up[low:high].astype(bf16)
            low = high

    @pl.when(j < count)
    def _():
        for c in copies(lax.rem(j, 2)):
            c.wait()

    @pl.when(j == 0)
    def _():
        fetch(lambda c: c.wait(), 0)


def product(place, blocks, pieces, weights, first, last, cuts, *tokens):
    block, depth = blocks[0].shape
    rows = 2 * len(pieces) * block
    count = last - first
    sizes = [high - low for low, high in zip((0,) + cuts[:-1], cuts)]
    anywhere = [pl.BlockSpec(memory_space=pl.ANY)]
    stay = [pl.BlockSpec(memory_space=pltpu.HBM)]

    def column(side):
        return pl.BlockSpec(
            (depth, 1, 2, 128),
            lambda j, _: (0, 2 * (first + jnp.minimum(j, count - 1)) + side, 0, 0),
        )

    return pl.pallas_call(
        functools.partial(product_kernel, count=count, cuts=cuts, pieces=pieces),
        grid_spec=pltpu.PrefetchScalarGridSpec(
            num_scalar_prefetch=1,
            grid=(count + 1,),
            in_specs=anywhere * len(blocks) + stay * len(tokens) + [column(0), column(1)],
            out_specs=[
                pl.BlockSpec((2, size, 256), lambda j, _: (0, 0, jnp.maximum(j - 1, 0)))
                for size in sizes
            ]
            + [token_spec()],
            scratch_shapes=[
                pltpu.VMEM((rows, depth), bf16),
                pltpu.SemaphoreType.DMA((2, 2)),
                pltpu.SemaphoreType.DMA((len(pieces), 2)),
                pltpu.VMEM((2, 2, 2 * depth, 128), bf16),
            ],
        ),
        out_shape=[jax.ShapeDtypeStruct((2, size, count * 256), bf16) for size in sizes] + [TOKEN],
        compiler_params=pltpu.CompilerParams(vmem_limit_bytes=VMEM),
        cost_estimate=SHORT,
    )(place, *blocks, *tokens, weights, weights)


def gated_kernel(swap_ref, held_ref, kept_ref, near_ref, far_ref, out_ref, token_ref):
    token_ref[...] = jnp.zeros_like(token_ref)
    half = near_ref.shape[1]
    for i, theirs in enumerate((near_ref, far_ref)):
        rows = slice(i * half, (i + 1) * half)
        gate = kept_ref[0, rows].astype(f32) + theirs[0].astype(f32)
        up = kept_ref[1, rows].astype(f32) + theirs[1].astype(f32)
        start = jnp.bitwise_xor(swap_ref[0], i) * half
        out_ref[pl.ds(pl.multiple_of(start, half), half), :] = (jax.nn.silu(gate) * up).astype(bf16)


def gated(kept, near, far, swap, held, first, width):
    rows, half, columns = kept.shape[1], near.shape[1], kept.shape[2]
    wide = 512 if columns % 512 == 0 and first % 2 == 0 else 256
    return pl.pallas_call(
        gated_kernel,
        grid_spec=pltpu.PrefetchScalarGridSpec(
            num_scalar_prefetch=1,
            grid=(columns // wide,),
            in_specs=[
                pl.BlockSpec(memory_space=pl.ANY),
                pl.BlockSpec((2, rows, wide), lambda j, _: (0, 0, j)),
                pl.BlockSpec((2, half, wide), lambda j, _: (0, 0, j)),
                pl.BlockSpec((2, half, wide), lambda j, _: (0, 0, j)),
            ],
            out_specs=[
                pl.BlockSpec((rows, wide), lambda j, _: (0, first * 256 // wide + j)),
                token_spec(),
            ],
        ),
        out_shape=[jax.ShapeDtypeStruct((rows, width), bf16), TOKEN],
        input_output_aliases={} if held is None else {1: 0},
        cost_estimate=SHORT,
    )(swap, kept if held is None else held, kept, near, far)


def on_device(prompt_rows, gate_up, queries, new_kv, kv_cache, lengths):
    gx, gy, gz = (lax.axis_index(a) for a in ("gx", "gy", "gz"))
    chips = lax.axis_size("gx")
    cores = lax.axis_size("gz")
    depth, _, width = gate_up.shape
    block = prompt_rows.shape[0]
    to_send = ((gx // 2) != gy).astype(jnp.int32)
    place = jnp.stack([gx, gz, to_send])
    over = [(0, 1), (1, 0)]

    mine = interleave_lanes(prompt_rows)
    along = lax.ppermute(mine, "gx", xor_pairs("gx", 2))
    mine_far = lax.ppermute(mine, "gx", xor_pairs("gx", 1))
    mine_other = lax.ppermute(mine, "gz", over)

    steps = queries.shape[0]
    sequences, slots = kv_cache.shape[:2]
    me = gx * cores + gz
    heads = queries.shape[2] // HD
    rows = steps * heads
    my_q = queries.reshape(steps, sequences, heads, HD).transpose(1, 0, 2, 3)
    my_q = after(my_q.reshape(1, sequences, rows, HD), mine)
    all_q = jnp.concatenate(
        [my_q] + [lax.ppermute(my_q, "gx", xor_pairs("gx", bit)) for bit in range(1, chips)], axis=0
    )
    other_q = lax.ppermute(all_q, "gz", over)
    limits = jnp.clip(lengths - me * slots, 0, slots)
    num, stat, _ = cached_attention(all_q, other_q, kv_cache, limits, place)

    along = after(along, num)
    along_other = lax.ppermute(along, "gz", over)
    along_far = lax.ppermute(along, "gx", xor_pairs("gx", 1))
    mine_far_other = lax.ppermute(mine_far, "gz", over)
    along_far_other = lax.ppermute(along_far, "gz", over)

    other_num = lax.ppermute(num[1], "gz", over)
    other_stat = lax.ppermute(stat[1], "gz", over)
    pair, _ = join_pair(num, other_num, stat, other_stat)
    nums = [pair[0]]
    for bit in range(1, chips):
        nums.append(lax.ppermute(pair[bit], "gx", xor_pairs("gx", bit)))
    units = new_kv.reshape(steps, sequences, 2 * KVH, HD)
    keys = lax.dynamic_index_in_dim(units, gx, 2, False)
    values = lax.dynamic_index_in_dim(units, gx + KVH, 2, False)
    attended = join_all(nums, my_q[0], keys, values)

    weights = gate_up.reshape(depth, 2, width // 128, 128).transpose(0, 2, 1, 3)
    pairs = width // 256
    cuts = [0, pairs // 14 * 4, pairs // 14 * 10, pairs] if pairs % 14 == 0 else [0, pairs]
    spans = list(zip(cuts[:-1], cuts[1:]))
    half = cores * block
    swap = (gx % 2).reshape(1)
    near, tokens = [], (num,)
    blocks = (mine, mine_other, along, along_other)
    pieces = (((0, 1), (2, 3)),)
    for first, last in spans:
        out, done = product(place, blocks, pieces, weights, first, last, (half,), *tokens)
        near.append(lax.ppermute(out, "gy", over))
        tokens = (out, pair)
    blocks += (mine_far, mine_far_other, along_far, along_far_other)
    pieces = (((4, 5), (6, 7)), ((2, 3), (0, 1)), ((6, 7), (4, 5)))
    tokens = (out, near[0])
    hidden_units = None
    waiting = []
    for i, (first, last) in enumerate(spans):
        sent, keep, done = product(
            place, blocks, pieces, weights, first, last, (half, 3 * half), *tokens
        )
        waiting.append((keep, near[i], lax.ppermute(sent, "gy", over), first))
        tokens = (done, near[1], *nums[1:]) if i == 0 else (done, near[-1])
        if i + 1 >= len(spans) - 1 and len(waiting) > 1:
            keep, early, late, start = waiting.pop(0)
            hidden_units, done = gated(keep, early, late, swap, hidden_units, start, width)
            tokens += (done,)
    for keep, early, late, start in waiting:
        hidden_units, _ = gated(keep, early, late, swap, hidden_units, start, width)

    attended = attended.reshape(sequences, steps, heads, HD).transpose(1, 0, 2, 3)
    return hidden_units, attended.reshape(steps, sequences, heads * HD)


def plain_on_device(prompt_rows, gate_up, queries, new_kv, kv_cache, lengths):
    partial_terms = jnp.dot(
        lax.all_gather(prompt_rows, ("gx", "gz"), axis=0, tiled=True),
        gate_up.reshape(gate_up.shape[0], -1),
        preferred_element_type=f32,
    )
    summed = lax.psum_scatter(
        partial_terms.astype(bf16), "gy", scatter_dimension=0, tiled=True
    ).astype(f32)
    summed = summed.reshape(summed.shape[0], 2, -1)
    hidden_units = (jax.nn.silu(summed[:, 0]) * summed[:, 1]).astype(bf16)
    members = lax.axis_size(("gx", "gz"))
    me = lax.axis_index(("gx", "gz"))
    steps = queries.shape[0]
    sequences, slots = kv_cache.shape[:2]
    all_q = lax.all_gather(queries, ("gx", "gz"), axis=2, tiled=True)
    grouped = all_q.reshape(steps, sequences, KVH, -1, HD)
    cache = kv_cache.reshape(sequences, slots, 2, KVH, HD)
    fresh = new_kv.reshape(steps, sequences, 2, KVH, HD).transpose(1, 0, 2, 3, 4)
    units = jnp.concatenate([cache, fresh], axis=1)
    scores = jnp.einsum(
        "sukgd,ujkd->sukgj", grouped, units[:, :, 0], preferred_element_type=f32
    ) * (1.0 / math.sqrt(HD))
    cached = me * slots + jnp.arange(slots, dtype=jnp.int32)[None, :] < lengths[:, None]
    ids = jnp.arange(steps, dtype=jnp.int32)
    fresh_seen = (ids[None, :] <= ids[:, None]) & (me == 0)
    seen = jnp.concatenate(
        [
            jnp.broadcast_to(cached[None], (steps, sequences, slots)),
            jnp.broadcast_to(fresh_seen[:, None, :], (steps, sequences, steps)),
        ],
        axis=2,
    )[:, :, None, None, :]
    masked = jnp.where(seen, scores, lowest)
    top = jnp.max(masked, axis=-1)
    probs = jnp.where(seen, jnp.exp(masked - top[..., None]), 0.0)
    den = jnp.sum(probs, axis=-1)
    num = jnp.einsum(
        "sukgj,ujkd->sukgd", probs.astype(bf16), units[:, :, 1], preferred_element_type=f32
    )
    overall = lax.pmax(top, ("gx", "gz"))
    scale = jnp.exp(top - overall)
    num = (num * scale[..., None]).reshape(steps, sequences, -1, HD)
    den = (den * scale).reshape(steps, sequences, -1)
    num = lax.psum_scatter(
        num.astype(bf16), ("gx", "gz"), scatter_dimension=2, tiled=True
    ).astype(f32)
    den = lax.psum_scatter(den, ("gx", "gz"), scatter_dimension=2, tiled=True)
    attended = (num / den[..., None]).astype(bf16)
    return hidden_units, attended.reshape(steps, sequences, -1)


def solution(mesh):
    sizes = mesh.shape
    paired = sizes["gy"] == 2 and sizes["gx"] == KVH and sizes["gz"] == 2
    return jax.shard_map(
        on_device if paired else plain_on_device,
        mesh=mesh,
        in_specs=(
            P(("groups", "gx", "gz"), "gy"),
            P("gy", None, ("gx", "gz")),
            P(None, ("groups", "gy"), ("gx", "gz")),
            P(None, ("groups", "gy"), None),
            P(("groups", "gy"), ("gx", "gz"), None),
            P(("groups", "gy")),
        ),
        out_specs=(P(("groups", "gy"), ("gx", "gz")), P(None, ("groups", "gy"), ("gx", "gz"))),
        check_vma=False,
    )
```
